512 devices in a mesh: ma: 128 (over y, x, z_lo), af: 4 (over z_hi, core).
Axes of the slice: x: 4, y: 4, z: 16 (z_hi: 2, z_lo: 8; z = z_hi * 8 + z_lo), core: 2. Of those that a mesh axis runs over, the one named last changes fastest.
Arguments:
- visibilities: bfloat16 [4096, 16, 2, 2000], P('ma', 'af'), may hold values from -6 to 6
- kl_basis: bfloat16 [128, 16, 2, 2000, 128], P('ma', 'af'), may hold values from -0.109375 to 0.109375
- eigenvalues: float32 [128, 128], P('ma'), may hold values from 0.1 to 100
- kept_modes: int32 [128], P('ma'), may hold values from 32 to 128, as said below
- assigned_m: int32 [128], replicated, may hold values from 0 to 4095, as said below
Outputs:
- kl_coeffs: float32 [128, 128], P('ma')
- cleaned: float32 [128, 16, 2, 2000], P('ma', 'af')
The draws below stay inside these ranges and needn't reach their ends.
Inputs may be any that keep to these rules, and one draw needn't show every extreme that they name: `kept_modes`: both ends are taken by some entry. `assigned_m`: 128 distinct values; 0 and 4095 are among them.
All inputs are finite; a program needn't handle non-finite values.
Results may differ from the reference program's by a relative error of at most 0.0037.
Values may be sent and summed in bfloat16 or wider, within the bound.
A program may use at most 64 MiB of HBM per device.

```python
import math
import jax
import jax.numpy as jnp
from jax import lax

RA = 4096
B = 2000
F = 16
KL = 128
M = 128


def draw_assigned_m(key, part):
    key = jax.random.fold_in(key, 11)
    leading, second = jax.random.split(key)
    chosen = jax.random.permutation(leading, RA - 2)[:M] + 1
    positions = jax.random.permutation(second, M)
    chosen = chosen.at[positions[0]].set(0).at[positions[1]].set(RA - 1)
    return chosen.astype(jnp.int32)


def draw_kept_modes(key, part):
    key = jax.random.fold_in(key, 23)
    leading, second = jax.random.split(key)
    counts = jax.random.randint(leading, (M,), KL // 4, KL + 1)
    positions = jax.random.permutation(second, M)
    counts = counts.at[positions[0]].set(KL).at[positions[1]].set(KL // 4)
    return counts.astype(jnp.int32)


def steps_of(rng, dims, cuts, low, largest):
    loudness = 1.0
    for position, parts in cuts:
        steps = jax.random.uniform(jax.random.fold_in(jax.random.fold_in(rng, 6), position), (parts,), jnp.float32, low / len(cuts), largest / len(cuts))
        loudness = loudness * jnp.repeat(jnp.exp(steps), dims[position] // parts).reshape((-1,) + (1,) * (len(dims) - 1 - position))
    return loudness


def gaussian(own_key, dims, scale, most, shards=(), held_as=jnp.bfloat16):
    entries = jax.random.normal(own_key, dims, jnp.float32) * scale
    if len(shards) > 0:
        entries = steps_of(own_key, dims, shards, -0.22, 0.18) * entries
    return jnp.clip(entries, min=-most, max=most).astype(held_as)


def setup_inputs(seed: int = 0) -> dict:
    seeds = jax.random.split(jax.random.key(seed), 6)
    return {
        "visibilities": gaussian(seeds[0], (RA, F, 2, B), 1.0, 6.0, ((0, 128), (1, 4))),
        "kl_basis": gaussian(seeds[1], (M, F, 2, B, KL), 2862 ** -0.5, 0.109375, ((0, 128), (1, 4))),
        "eigenvalues": jnp.clip(jnp.exp(math.log(100.0) - 6.9077553 * jax.random.uniform(seeds[2], (M, KL), jnp.float32) ** steps_of(seeds[2], (M, KL), ((0, 128),), -0.2, 0.2)), 0.1, 100.0),
        "kept_modes": draw_kept_modes(jax.random.fold_in(seeds[5], 71), 0),
        "assigned_m": draw_assigned_m(jax.random.fold_in(seeds[5], 71), 0),
    }


def dft_table(assigned_m, length):
    offsets = jnp.arange(length, dtype=jnp.int32)
    phase = assigned_m.astype(jnp.int32)[:, None] * offsets[None, :] % length
    angles = phase.astype(jnp.float32) * (2.0 * math.pi / length)
    factor = 1.0 / math.sqrt(length)
    return jnp.stack([jnp.cos(angles) * factor, -jnp.sin(angles) * factor]).astype(jnp.bfloat16)

def combine(device_parts):
    real_part = device_parts[0][..., 0, :] - device_parts[1][..., 1, :]
    imag_part = device_parts[0][..., 1, :] + device_parts[1][..., 0, :]
    return jnp.stack([real_part, imag_part], axis=-2)

def reference(visibilities, kl_basis, eigenvalues, kept_modes, assigned_m):
    dft_matrix = dft_table(assigned_m, RA).astype(jnp.float32).reshape(2 * M, RA)

    def one_channel(channel):
        columns = channel.astype(jnp.float32).reshape(RA, 2 * B)
        sums = jnp.dot(dft_matrix, columns, precision=lax.Precision.HIGHEST)
        return combine(sums.reshape(2, M, 2, B))
    power_spectrum = lax.map(one_channel, jnp.moveaxis(visibilities, 1, 0))
    power_spectrum = jnp.moveaxis(power_spectrum, 0, 1)
    keep_mask = (jnp.arange(KL, dtype=jnp.int32)[None, :] < kept_modes[:, None]).astype(jnp.float32)
    gains = eigenvalues / (1.0 + eigenvalues) * keep_mask

    def one_mode(item):
        vector, basis, gain_row = item
        matrix = basis.astype(jnp.float32)
        rounded = lax.optimization_barrier(vector.astype(jnp.bfloat16)).astype(jnp.float32)
        projection = jnp.dot(rounded, matrix, precision=lax.Precision.HIGHEST)
        coeffs = projection * gain_row
        half = lax.optimization_barrier(coeffs.astype(jnp.bfloat16)).astype(jnp.float32)
        restored_visibilities = jnp.dot(matrix, half, precision=lax.Precision.HIGHEST)
        return (coeffs, vector - restored_visibilities)
    coeffs, cleaned = lax.map(one_mode, (power_spectrum.reshape(M, F * 2 * B), kl_basis.reshape(M, F * 2 * B, KL), gains))
    return (coeffs, cleaned.reshape(M, F, 2, B))
```

```python
import functools
import math

import jax
import jax.numpy as jnp
from jax import lax
from jax.experimental import pallas as pl
from jax.experimental.pallas import tpu as pltpu
from jax.sharding import PartitionSpec as P

MESH = pl.DeviceIdType.MESH
Z = 8
SIDE = 4
YX = SIDE * SIDE
LANES = 128
WIDTH = 256
AHEAD = 2
FARTHEST_FIRST = (4, 3, 5, 2, 6, 1, 7)
LEVELS = 32767.0
AHEAD = 2


def dft_block(m_column, row_shift, column_start, z, length, ra_per_device):
    rows = m_column.shape[0]
    column = lax.broadcasted_iota(jnp.int32, (rows, LANES), 1) + column_start
    part = column & 1
    per_source = 2 * ra_per_device
    source = column // per_source
    within = (column - source * per_source) >> 1
    t = source * (Z * ra_per_device) + z * ra_per_device + within
    quarter = length // 4
    phase = (m_column * t + (row_shift - part) * quarter) & (length - 1)
    wrapped = ((phase + length // 2) & (length - 1)) - length // 2
    u = quarter - jnp.abs(wrapped)
    x = u.astype(jnp.float32) * (2.0 * math.pi / length)
    x2 = x * x
    poly = jnp.float32(-1.0 / math.factorial(11))
    for order in (9, 7, 5, 3, 1):
        sign = 1.0 if order % 4 == 1 else -1.0
        poly = poly * x2 + jnp.float32(sign / math.factorial(order))
    return (x * poly * (1.0 / math.sqrt(length))).astype(jnp.bfloat16)


def kernel(
    length,
    vis,
    basis,
    eigen,
    kept,
    assigned,
    coeff_out,
    clean_out,
    recv,
    tail,
    table,
    part,
    zq,
    zs,
    zqr,
    zsr,
    fsend,
    spec,
    basis_v,
    proj,
    eigen_v,
    assigned_v,
    basis_sem,
    small_sem,
    p1_send,
    p1_recv,
    zq_send,
    zq_recv,
    zs_send,
    zs_recv,
    f_send,
    f_recv,
    a_send,
    a_recv,
    answer,
):
    chunks, _, ra, _, _ = recv.shape
    nf, _, width = vis.shape[1:]
    quarter_width = chunks * WIDTH
    tail_width = tail.shape[-1]
    per_f = YX // nf
    ma = lax.axis_index("ma")
    af = lax.axis_index("af")
    yx = ma // Z
    z = ma % Z
    y, x = yx // SIDE, yx % SIDE

    def at_yx(other):
        return (other * Z + z, af)

    def at_z(other):
        return (yx * Z + other, af)

    def peer(step):
        dy, dx = step // SIDE, step % SIDE
        return ((y + dy) % SIDE) * SIDE + (x + dx) % SIDE

    def source(step):
        dy, dx = step // SIDE, step % SIDE
        return ((y + SIDE - dy) % SIDE) * SIDE + (x + SIDE - dx) % SIDE

    basis_copy = pltpu.make_async_copy(basis, basis_v, basis_sem)
    small_copies = [
        pltpu.make_async_copy(assigned, assigned_v, small_sem.at[0]),
        pltpu.make_async_copy(eigen, eigen_v, small_sem.at[1]),
    ]
    for copy in small_copies:
        copy.start()

    barrier = pltpu.get_barrier_semaphore()
    half, core = af // 2, af % 2
    role = jnp.where(z < Z // 2, 1 - half, half)
    far = [(ma, (1 - half) * 2 + d) for d in (0, 1)]
    partners = [(ma, half * 2 + 1 - core)]
    partners += [at_z((z + d) % Z) for d in range(1, Z)]
    partners += [at_yx(peer(s)) for s in range(1, YX)]
    @pl.when(role == 1)
    def _():
        for partner in far:
            pl.semaphore_signal(barrier, inc=1, device_id=partner, device_id_type=MESH)

    for partner in partners:
        pl.semaphore_signal(barrier, inc=1, device_id=partner, device_id_type=MESH)

    def window(dest, k, wide):
        f, piece = dest // per_f, dest % per_f
        start = pl.multiple_of(piece * quarter_width + k * WIDTH, LANES)
        return vis.at[:, f, :, pl.ds(start, wide)]

    tail_start = (per_f - 1) * quarter_width + (chunks - 1) * WIDTH

    def tail_window(dest):
        return vis.at[:, dest // per_f, :, pl.ds(tail_start, tail_width)]

    is_tail = yx % per_f == per_f - 1
    for k in range(chunks):
        if k < chunks - 1:
            pltpu.make_async_copy(window(yx, k, WIDTH), recv.at[k, yx], p1_recv.at[k]).start()
        else:

            @pl.when(is_tail)
            def _():
                pltpu.make_async_copy(tail_window(yx), tail.at[yx], p1_recv.at[k]).start()

            @pl.when(jnp.logical_not(is_tail))
            def _():
                pltpu.make_async_copy(
                    window(yx, k, WIDTH), recv.at[k, yx], p1_recv.at[k]
                ).start()

    def each_piece(k, act, steps=tuple(range(1, YX))):
        for step in steps:
            if k < chunks - 1:
                act(step, k, False)
            else:
                to_tail = peer(step) % per_f == per_f - 1

                @pl.when(to_tail)
                def _():
                    act(step, k, True)

                @pl.when(jnp.logical_not(to_tail))
                def _():
                    act(step, k, False)

    @pl.when(role == 1)
    def _():
        pl.semaphore_wait(barrier, len(partners))

    @pl.when(role == 0)
    def _():
        pl.semaphore_wait(barrier, len(partners) + len(far))
        for partner in far:
            pl.semaphore_signal(answer, inc=1, device_id=partner, device_id_type=MESH)

    def p1(step, k, tailed):
        dest = peer(step)
        if tailed:
            src, dst = tail_window(dest), tail.at[yx]
        else:
            src, dst = window(dest, k, WIDTH), recv.at[k, yx]
        return pltpu.make_async_remote_copy(
            src_ref=src,
            dst_ref=dst,
            send_sem=p1_send.at[k, int(tailed)],
            recv_sem=p1_recv.at[k],
            device_id=at_yx(dest),
            device_id_type=MESH,
        )

    for k in range(min(AHEAD, chunks)):
        each_piece(k, lambda step, k, tailed: p1(step, k, tailed).start())

    basis_copy.start()

    rows = table.shape[0]
    row = lax.broadcasted_iota(jnp.int32, (rows, LANES), 0)
    lane = lax.broadcasted_iota(jnp.int32, (rows, LANES), 1)
    block = 2 * YX
    index = ((row % block) // 2) * Z + row // block
    small_copies[0].wait()
    chosen = jnp.where(lane == index, assigned_v[...].astype(jnp.float32), 0.0)
    m_column = jnp.sum(chosen, axis=1, keepdims=True).astype(jnp.int32)
    row_shift = row[:, :1] & 1
    for j in range(table.shape[1] // LANES):
        table[:, j * LANES : (j + 1) * LANES] = dft_block(
            m_column, row_shift, j * LANES, z, length, ra
        )

    def z_copies(d, k):
        target = dict(device_id=at_z((z + d) % Z), device_id_type=MESH)
        return [
            pltpu.make_async_remote_copy(
                src_ref=src.at[k, (z + d) % Z],
                dst_ref=dst.at[k, d - 1],
                send_sem=send.at[k],
                recv_sem=recv.at[k],
                **target,
            )
            for src, dst, send, recv in (
                (zs, zsr, zs_send, zs_recv),
                (zq, zqr, zq_send, zq_recv),
            )
        ]

    def rows_of(other):
        return pl.ds(pl.multiple_of(other * block, block), block)

    def arrived(ref, sem):
        pltpu.make_async_copy(ref, ref, sem).wait()

    def transform(k):
        def whole():
            arrived(recv.at[k], p1_recv.at[k])
            columns = recv[k].reshape(YX * 2 * ra, WIDTH)
            part[k] = jnp.dot(table[...], columns, preferred_element_type=jnp.float32)

        if k < chunks - 1:
            whole()
        else:

            @pl.when(is_tail)
            def _():
                arrived(tail, p1_recv.at[k])
                columns = tail[...].reshape(YX * 2 * ra, tail_width)
                part[k] = jnp.zeros_like(part[k])
                part[k, :, 0:tail_width] = jnp.dot(
                    table[...], columns, preferred_element_type=jnp.float32
                )

            @pl.when(jnp.logical_not(is_tail))
            def _():
                whole()

        pieces = part[k].reshape(Z, block, WIDTH)
        largest = jnp.maximum(jnp.max(jnp.abs(pieces), axis=1, keepdims=True), 1e-30)
        zs[k] = largest * (1.0 / LEVELS)
        zq[k] = jnp.round(pieces * (LEVELS / largest)).astype(jnp.int32).astype(jnp.int16)
        per_message = -(-(YX - 1) // (Z - 1))
        for i, d in enumerate(FARTHEST_FIRST):
            for copy in z_copies(d, k):
                copy.start()
            if k + AHEAD < chunks:
                each_piece(
                    k + AHEAD,
                    lambda step, k, tailed: p1(step, k, tailed).start(),
                    range(1, YX)[i * per_message : (i + 1) * per_message],
                )

    def place(src, k):
        start = pl.multiple_of((src % per_f) * quarter_width + k * WIDTH, LANES)
        return spec.at[src // per_f, :, pl.ds(start, WIDTH)]

    def f_local(k):
        return pltpu.make_async_copy(fsend.at[k, yx], place(yx, k), f_recv.at[k])

    def f_copy(step, k):
        dest = peer(step)
        return pltpu.make_async_remote_copy(
            src_ref=fsend.at[k, dest],
            dst_ref=place(yx, k),
            send_sem=f_send.at[k],
            recv_sem=f_recv.at[k],
            device_id=at_yx(dest),
            device_id_type=MESH,
        )

    def reduce(k):
        total = part[k, rows_of(z)]
        arrived(zsr.at[k], zs_recv.at[k])
        arrived(zqr.at[k], zq_recv.at[k])
        for d in FARTHEST_FIRST:
            total += zqr[k, d - 1].astype(jnp.float32) * zsr[k, d - 1]
        fsend[k] = total.reshape(YX, 2, WIDTH)
        f_local(k).start()
        for step in range(1, YX):
            f_copy(step, k).start()

    for k in range(chunks + 1):
        if k < chunks:
            transform(k)
        if k >= 1:
            reduce(k - 1)

    basis_copy.wait()
    total = jnp.zeros((1, LANES), jnp.float32)
    for k in range(chunks):
        arrived(fsend.at[k], f_recv.at[k])
        for piece in range(per_f):
            start = piece * quarter_width + k * WIDTH
            stop = min(start + WIDTH, width)
            for f in range(nf):
                for c in range(2):
                    rounded = spec[f, c : c + 1, start:stop].astype(jnp.bfloat16)
                    total += jnp.dot(
                        rounded, basis_v[f, c, start:stop], preferred_element_type=jnp.float32
                    )
    proj[af] = total

    def a_copy(d):
        return pltpu.make_async_remote_copy(
            src_ref=proj.at[af],
            dst_ref=proj.at[af],
            send_sem=a_send.at[d - 1],
            recv_sem=a_recv.at[d - 1],
            device_id=(ma, (af + d) % 4),
            device_id_type=MESH,
        )

    @pl.when(role == 1)
    def _():
        pl.semaphore_wait(answer, len(far))

    for d in (1, 2, 3):
        a_copy(d).start()
    for k in range(chunks):
        if k < chunks - 1:
            arrived(recv.at[k, pl.ds(0, YX - 1)], p1_send.at[k, 0])
        else:

            @pl.when(is_tail)
            def _():
                arrived(recv.at[k, pl.ds(0, YX - nf)], p1_send.at[k, 0])
                arrived(tail.at[pl.ds(0, nf - 1)], p1_send.at[k, 1])

            @pl.when(jnp.logical_not(is_tail))
            def _():
                arrived(recv.at[k, pl.ds(0, YX - nf - 1)], p1_send.at[k, 0])
                arrived(tail.at[pl.ds(0, nf)], p1_send.at[k, 1])

        arrived(zsr.at[k], zs_send.at[k])
        arrived(zqr.at[k], zq_send.at[k])
        arrived(fsend.at[k, pl.ds(0, YX - 1)], f_send.at[k])
    for d in (1, 2, 3):
        a_copy(d).wait_recv()
    summed = proj[0] + proj[1] + proj[2] + proj[3]
    lanes = lax.broadcasted_iota(jnp.int32, (1, LANES), 1)
    small_copies[1].wait()
    keep = jnp.where(lanes < kept[0], 1.0, 0.0)
    gains = eigen_v[...] / (1.0 + eigen_v[...]) * keep
    coeffs = summed * gains
    coeff_out[...] = coeffs
    half_coeffs = coeffs.astype(jnp.bfloat16)
    for f in range(nf):
        for c in range(2):
            restored = lax.dot_general(
                half_coeffs,
                basis_v[f, c],
                (((1,), (1,)), ((), ())),
                preferred_element_type=jnp.float32,
            )
            clean_out[f, c : c + 1, :] = spec[f, c : c + 1, 0:width] - restored

    for d in (1, 2, 3):
        a_copy(d).wait_send()


def local(visibilities, kl_basis, eigenvalues, kept_modes, assigned_m):
    ra, nf, _, width = visibilities.shape
    length = ra * YX * Z
    modes = kl_basis.shape[-1]
    per_f = YX // nf
    chunks = -(-width // (per_f * WIDTH))
    tail_width = width - (per_f * chunks - 1) * WIDTH
    rows = 2 * assigned_m.shape[0]
    block = 2 * YX
    f32 = jnp.float32
    dma = pltpu.SemaphoreType.DMA
    vmem, smem, hbm = pltpu.VMEM, pltpu.SMEM, pltpu.HBM
    in_hbm = functools.partial(pltpu.with_memory_space_constraint, memory_space=hbm)
    coeffs, cleaned = pl.pallas_call(
        functools.partial(kernel, length),
        out_shape=(
            vmem((1, modes), f32),
            vmem((nf, 2, width), f32),
        ),
        in_specs=[pl.BlockSpec(memory_space=s) for s in (hbm, hbm, hbm, smem, hbm)],
        out_specs=(pl.BlockSpec(memory_space=vmem), pl.BlockSpec(memory_space=vmem)),
        scratch_shapes=[
            vmem((chunks, YX, ra, 2, WIDTH), jnp.bfloat16),
            vmem((YX, ra, 2, tail_width), jnp.bfloat16),
            vmem((rows, YX * ra * 2), jnp.bfloat16),
            vmem((chunks, rows, WIDTH), f32),
            vmem((chunks, Z, block, WIDTH), jnp.int16),
            vmem((chunks, Z, 1, WIDTH), f32),
            vmem((chunks, Z - 1, block, WIDTH), jnp.int16),
            vmem((chunks, Z - 1, 1, WIDTH), f32),
            vmem((chunks, YX, 2, WIDTH), f32),
            vmem((nf, 2, per_f * chunks * WIDTH), f32),
            vmem((nf, 2, width, modes), jnp.bfloat16),
            vmem((4, 1, modes), f32),
            vmem((1, modes), f32),
            vmem((1, rows // 2), jnp.int32),
            dma,
            dma((2,)),
            dma((chunks, 2)),
            dma((chunks,)),
            dma((chunks,)),
            dma((chunks,)),
            dma((chunks,)),
            dma((chunks,)),
            dma((chunks,)),
            dma((chunks,)),
            dma((3,)),
            dma((3,)),
            pltpu.SemaphoreType.REGULAR,
        ],
        compiler_params=pltpu.CompilerParams(
            collective_id=0, has_side_effects=True, vmem_limit_bytes=40 << 20
        ),
    )(
        in_hbm(visibilities),
        in_hbm(kl_basis.reshape(nf, 2, width, modes)),
        in_hbm(eigenvalues),
        kept_modes,
        in_hbm(assigned_m.reshape(1, -1)),
    )
    return coeffs, cleaned[None]


def solution(mesh):
    in_specs = (
        P("ma", "af", None, None),
        P("ma", "af", None, None, None),
        P("ma", None),
        P("ma"),
        P(),
    )
    out_specs = (P("ma", None), P("ma", "af", None, None))
    return jax.shard_map(local, mesh=mesh, in_specs=in_specs, out_specs=out_specs, check_vma=False)
```

```python
import functools
import math

import jax
import jax.numpy as jnp
from jax import lax
from jax.experimental import pallas as pl
from jax.experimental.pallas import tpu as pltpu
from jax.sharding import PartitionSpec as P

MESH = pl.DeviceIdType.MESH
Z = 8
SIDE = 4
YX = SIDE * SIDE
LANES = 128
WIDTH = 256
AHEAD = 2
Z_STEPS = (1, 2, 3, 4, 5, 6, 7)
LEVELS = 32767.0
AHEAD = 2


def dft_block(m_column, row_shift, column_start, z, length, ra_per_device):
    rows = m_column.shape[0]
    column = lax.broadcasted_iota(jnp.int32, (rows, LANES), 1) + column_start
    part = column & 1
    per_source = 2 * ra_per_device
    source = column // per_source
    within = (column - source * per_source) >> 1
    t = source * (Z * ra_per_device) + z * ra_per_device + within
    quarter = length // 4
    phase = (m_column * t + (row_shift - part) * quarter) & (length - 1)
    wrapped = ((phase + length // 2) & (length - 1)) - length // 2
    u = quarter - jnp.abs(wrapped)
    x = u.astype(jnp.float32) * (2.0 * math.pi / length)
    x2 = x * x
    poly = jnp.float32(-1.0 / math.factorial(11))
    for order in (9, 7, 5, 3, 1):
        sign = 1.0 if order % 4 == 1 else -1.0
        poly = poly * x2 + jnp.float32(sign / math.factorial(order))
    return (x * poly * (1.0 / math.sqrt(length))).astype(jnp.bfloat16)


def kernel(
    length,
    vis,
    basis,
    eigen,
    kept,
    assigned,
    coeff_out,
    clean_out,
    recv,
    tail,
    table,
    part,
    zq,
    zs,
    zqr,
    zsr,
    fsend,
    spec,
    basis_v,
    basis_t,
    proj,
    eigen_v,
    assigned_v,
    basis_sem,
    small_sem,
    p1_send,
    p1_recv,
    zq_send,
    zq_recv,
    zs_send,
    zs_recv,
    f_send,
    f_recv,
    a_send,
    a_recv,
    answer,
):
    chunks, _, ra, _, _ = recv.shape
    nf, _, width = vis.shape[1:]
    quarter_width = chunks * WIDTH
    tail_width = tail.shape[-1]
    per_f = YX // nf
    ma = lax.axis_index("ma")
    af = lax.axis_index("af")
    yx = ma // Z
    z = ma % Z
    y, x = yx // SIDE, yx % SIDE

    def at_yx(other):
        return (other * Z + z, af)

    def at_z(other):
        return (yx * Z + other, af)

    def peer(step):
        dy, dx = step // SIDE, step % SIDE
        return ((y + dy) % SIDE) * SIDE + (x + dx) % SIDE

    def source(step):
        dy, dx = step // SIDE, step % SIDE
        return ((y + SIDE - dy) % SIDE) * SIDE + (x + SIDE - dx) % SIDE

    basis_copy = pltpu.make_async_copy(basis, basis_v, basis_sem)
    small_copies = [
        pltpu.make_async_copy(assigned, assigned_v, small_sem.at[0]),
        pltpu.make_async_copy(eigen, eigen_v, small_sem.at[1]),
    ]
    for copy in small_copies:
        copy.start()

    barrier = pltpu.get_barrier_semaphore()
    half, core = af // 2, af % 2
    role = jnp.where(z < Z // 2, 1 - half, half)
    far = [(ma, (1 - half) * 2 + d) for d in (0, 1)]
    partners = [(ma, half * 2 + 1 - core)]
    partners += [at_z((z + d) % Z) for d in range(1, Z)]
    partners += [at_yx(peer(s)) for s in range(1, YX)]
    @pl.when(role == 1)
    def _():
        for partner in far:
            pl.semaphore_signal(barrier, inc=1, device_id=partner, device_id_type=MESH)

    for partner in partners:
        pl.semaphore_signal(barrier, inc=1, device_id=partner, device_id_type=MESH)

    def window(dest, k, wide):
        f, piece = dest // per_f, dest % per_f
        start = pl.multiple_of(piece * quarter_width + k * WIDTH, LANES)
        return vis.at[:, f, :, pl.ds(start, wide)]

    tail_start = (per_f - 1) * quarter_width + (chunks - 1) * WIDTH

    def tail_window(dest):
        return vis.at[:, dest // per_f, :, pl.ds(tail_start, tail_width)]

    is_tail = yx % per_f == per_f - 1
    for k in range(chunks):
        if k < chunks - 1:
            pltpu.make_async_copy(window(yx, k, WIDTH), recv.at[k, yx], p1_recv.at[k]).start()
        else:

            @pl.when(is_tail)
            def _():
                pltpu.make_async_copy(tail_window(yx), tail.at[yx], p1_recv.at[k]).start()

            @pl.when(jnp.logical_not(is_tail))
            def _():
                pltpu.make_async_copy(
                    window(yx, k, WIDTH), recv.at[k, yx], p1_recv.at[k]
                ).start()

    def each_piece(k, act, steps=tuple(range(1, YX))):
        for step in steps:
            if k < chunks - 1:
                act(step, k, False)
            else:
                to_tail = peer(step) % per_f == per_f - 1

                @pl.when(to_tail)
                def _():
                    act(step, k, True)

                @pl.when(jnp.logical_not(to_tail))
                def _():
                    act(step, k, False)

    @pl.when(role == 1)
    def _():
        pl.semaphore_wait(barrier, len(partners))

    @pl.when(role == 0)
    def _():
        pl.semaphore_wait(barrier, len(partners) + len(far))
        for partner in far:
            pl.semaphore_signal(answer, inc=1, device_id=partner, device_id_type=MESH)

    def p1(step, k, tailed):
        dest = peer(step)
        if tailed:
            src, dst = tail_window(dest), tail.at[yx]
        else:
            src, dst = window(dest, k, WIDTH), recv.at[k, yx]
        return pltpu.make_async_remote_copy(
            src_ref=src,
            dst_ref=dst,
            send_sem=p1_send.at[k, int(tailed)],
            recv_sem=p1_recv.at[k],
            device_id=at_yx(dest),
            device_id_type=MESH,
        )

    for k in range(min(AHEAD, chunks)):
        each_piece(k, lambda step, k, tailed: p1(step, k, tailed).start())

    basis_copy.start()

    rows = table.shape[0]
    row = lax.broadcasted_iota(jnp.int32, (rows, LANES), 0)
    lane = lax.broadcasted_iota(jnp.int32, (rows, LANES), 1)
    block = 2 * YX
    index = ((row % block) // 2) * Z + row // block
    small_copies[0].wait()
    chosen = jnp.where(lane == index, assigned_v[...].astype(jnp.float32), 0.0)
    m_column = jnp.sum(chosen, axis=1, keepdims=True).astype(jnp.int32)
    row_shift = row[:, :1] & 1
    for j in range(table.shape[1] // LANES):
        table[:, j * LANES : (j + 1) * LANES] = dft_block(
            m_column, row_shift, j * LANES, z, length, ra
        )

    basis_copy.wait()
    for f in range(nf):
        for c in range(2):
            basis_t[f, c] = basis_v[f, c].T

    def z_copies(d, k):
        target = dict(device_id=at_z((z + d) % Z), device_id_type=MESH)
        return [
            pltpu.make_async_remote_copy(
                src_ref=src.at[k, (z + d) % Z],
                dst_ref=dst.at[k, d - 1],
                send_sem=send.at[k],
                recv_sem=recv.at[k],
                **target,
            )
            for src, dst, send, recv in (
                (zs, zsr, zs_send, zs_recv),
                (zq, zqr, zq_send, zq_recv),
            )
        ]

    def rows_of(other):
        return pl.ds(pl.multiple_of(other * block, block), block)

    def arrived(ref, sem):
        pltpu.make_async_copy(ref, ref, sem).wait()

    def transform(k):
        def whole():
            arrived(recv.at[k], p1_recv.at[k])
            columns = recv[k].reshape(YX * 2 * ra, WIDTH)
            part[k] = jnp.dot(table[...], columns, preferred_element_type=jnp.float32)

        if k < chunks - 1:
            whole()
        else:

            @pl.when(is_tail)
            def _():
                arrived(tail, p1_recv.at[k])
                columns = tail[...].reshape(YX * 2 * ra, tail_width)
                part[k] = jnp.zeros_like(part[k])
                part[k, :, 0:tail_width] = jnp.dot(
                    table[...], columns, preferred_element_type=jnp.float32
                )

            @pl.when(jnp.logical_not(is_tail))
            def _():
                whole()

        pieces = part[k].reshape(Z, block, WIDTH)
        largest = jnp.maximum(jnp.max(jnp.abs(pieces), axis=1, keepdims=True), 1e-30)
        zs[k] = largest * (1.0 / LEVELS)
        zq[k] = jnp.round(pieces * (LEVELS / largest)).astype(jnp.int32).astype(jnp.int16)
        per_message = -(-(YX - 1) // (Z - 1))
        for i, d in enumerate(Z_STEPS):
            for copy in z_copies(d, k):
                copy.start()
            if k + AHEAD < chunks:
                each_piece(
                    k + AHEAD,
                    lambda step, k, tailed: p1(step, k, tailed).start(),
                    range(1, YX)[i * per_message : (i + 1) * per_message],
                )

    def place(src, k):
        start = pl.multiple_of((src % per_f) * quarter_width + k * WIDTH, LANES)
        return spec.at[src // per_f, :, pl.ds(start, WIDTH)]

    def f_local(k):
        return pltpu.make_async_copy(fsend.at[k, yx], place(yx, k), f_recv.at[k])

    def f_copy(step, k):
        dest = peer(step)
        return pltpu.make_async_remote_copy(
            src_ref=fsend.at[k, dest],
            dst_ref=place(yx, k),
            send_sem=f_send.at[k],
            recv_sem=f_recv.at[k],
            device_id=at_yx(dest),
            device_id_type=MESH,
        )

    def reduce(k):
        total = part[k, rows_of(z)]
        arrived(zsr.at[k], zs_recv.at[k])
        arrived(zqr.at[k], zq_recv.at[k])
        for d in Z_STEPS:
            total += zqr[k, d - 1].astype(jnp.float32) * zsr[k, d - 1]
        fsend[k] = total.reshape(YX, 2, WIDTH)
        f_local(k).start()
        for step in range(1, YX):
            f_copy(step, k).start()

    for k in range(chunks + 1):
        if k < chunks:
            transform(k)
        if k >= 1:
            reduce(k - 1)

    total = jnp.zeros((1, LANES), jnp.float32)
    for k in range(chunks):
        arrived(fsend.at[k], f_recv.at[k])
        for piece in range(per_f):
            start = piece * quarter_width + k * WIDTH
            stop = min(start + WIDTH, width)
            for f in range(nf):
                for c in range(2):
                    rounded = spec[f, c : c + 1, start:stop].astype(jnp.bfloat16)
                    total += jnp.dot(
                        rounded, basis_v[f, c, start:stop], preferred_element_type=jnp.float32
                    )
    proj[af] = total

    def a_copy(d):
        return pltpu.make_async_remote_copy(
            src_ref=proj.at[af],
            dst_ref=proj.at[af],
            send_sem=a_send.at[d - 1],
            recv_sem=a_recv.at[d - 1],
            device_id=(ma, (af + d) % 4),
            device_id_type=MESH,
        )

    @pl.when(role == 1)
    def _():
        pl.semaphore_wait(answer, len(far))

    for d in (1, 2, 3):
        a_copy(d).start()
    for k in range(chunks):
        if k < chunks - 1:
            arrived(recv.at[k, pl.ds(0, YX - 1)], p1_send.at[k, 0])
        else:

            @pl.when(is_tail)
            def _():
                arrived(recv.at[k, pl.ds(0, YX - nf)], p1_send.at[k, 0])
                arrived(tail.at[pl.ds(0, nf - 1)], p1_send.at[k, 1])

            @pl.when(jnp.logical_not(is_tail))
            def _():
                arrived(recv.at[k, pl.ds(0, YX - nf - 1)], p1_send.at[k, 0])
                arrived(tail.at[pl.ds(0, nf)], p1_send.at[k, 1])

        arrived(zsr.at[k], zs_send.at[k])
        arrived(zqr.at[k], zq_send.at[k])
        arrived(fsend.at[k, pl.ds(0, YX - 1)], f_send.at[k])
    for d in (1, 2, 3):
        a_copy(d).wait_recv()
    summed = proj[0] + proj[1] + proj[2] + proj[3]
    lanes = lax.broadcasted_iota(jnp.int32, (1, LANES), 1)
    small_copies[1].wait()
    keep = jnp.where(lanes < kept[0], 1.0, 0.0)
    gains = eigen_v[...] / (1.0 + eigen_v[...]) * keep
    coeffs = summed * gains
    coeff_out[...] = coeffs
    half_coeffs = coeffs.astype(jnp.bfloat16)
    for f in range(nf):
        for c in range(2):
            restored = jnp.dot(
                half_coeffs, basis_t[f, c], preferred_element_type=jnp.float32
            )
            clean_out[f, c : c + 1, :] = spec[f, c : c + 1, 0:width] - restored

    for d in (1, 2, 3):
        a_copy(d).wait_send()


def local(visibilities, kl_basis, eigenvalues, kept_modes, assigned_m):
    ra, nf, _, width = visibilities.shape
    length = ra * YX * Z
    modes = kl_basis.shape[-1]
    per_f = YX // nf
    chunks = -(-width // (per_f * WIDTH))
    tail_width = width - (per_f * chunks - 1) * WIDTH
    rows = 2 * assigned_m.shape[0]
    block = 2 * YX
    f32 = jnp.float32
    dma = pltpu.SemaphoreType.DMA
    vmem, smem, hbm = pltpu.VMEM, pltpu.SMEM, pltpu.HBM
    in_hbm = functools.partial(pltpu.with_memory_space_constraint, memory_space=hbm)
    coeffs, cleaned = pl.pallas_call(
        functools.partial(kernel, length),
        out_shape=(
            vmem((1, modes), f32),
            vmem((nf, 2, width), f32),
        ),
        in_specs=[pl.BlockSpec(memory_space=s) for s in (hbm, hbm, hbm, smem, hbm)],
        out_specs=(pl.BlockSpec(memory_space=vmem), pl.BlockSpec(memory_space=vmem)),
        scratch_shapes=[
            vmem((chunks, YX, ra, 2, WIDTH), jnp.bfloat16),
            vmem((YX, ra, 2, tail_width), jnp.bfloat16),
            vmem((rows, YX * ra * 2), jnp.bfloat16),
            vmem((chunks, rows, WIDTH), f32),
            vmem((chunks, Z, block, WIDTH), jnp.int16),
            vmem((chunks, Z, 1, WIDTH), f32),
            vmem((chunks, Z - 1, block, WIDTH), jnp.int16),
            vmem((chunks, Z - 1, 1, WIDTH), f32),
            vmem((chunks, YX, 2, WIDTH), f32),
            vmem((nf, 2, per_f * chunks * WIDTH), f32),
            vmem((nf, 2, width, modes), jnp.bfloat16),
            vmem((nf, 2, modes, width), jnp.bfloat16),
            vmem((4, 1, modes), f32),
            vmem((1, modes), f32),
            vmem((1, rows // 2), jnp.int32),
            dma,
            dma((2,)),
            dma((chunks, 2)),
            dma((chunks,)),
            dma((chunks,)),
            dma((chunks,)),
            dma((chunks,)),
            dma((chunks,)),
            dma((chunks,)),
            dma((chunks,)),
            dma((3,)),
            dma((3,)),
            pltpu.SemaphoreType.REGULAR,
        ],
        compiler_params=pltpu.CompilerParams(
            collective_id=0, has_side_effects=True, vmem_limit_bytes=40 << 20
        ),
    )(
        in_hbm(visibilities),
        in_hbm(kl_basis.reshape(nf, 2, width, modes)),
        in_hbm(eigenvalues),
        kept_modes,
        in_hbm(assigned_m.reshape(1, -1)),
    )
    return coeffs, cleaned[None]


def solution(mesh):
    in_specs = (
        P("ma", "af", None, None),
        P("ma", "af", None, None, None),
        P("ma", None),
        P("ma"),
        P(),
    )
    out_specs = (P("ma", None), P("ma", "af", None, None))
    return jax.shard_map(local, mesh=mesh, in_specs=in_specs, out_specs=out_specs, check_vma=False)
```

```python
import functools
import math

import jax
import jax.numpy as jnp
from jax import lax
from jax.experimental import pallas as pl
from jax.experimental.pallas import tpu as pltpu
from jax.sharding import PartitionSpec as P

MESH = pl.DeviceIdType.MESH
Z = 8
SIDE = 4
YX = SIDE * SIDE
LANES = 128
WIDTH = 256
AHEAD = 2
Z_STEPS = (1, 2, 3, 4, 5, 6, 7)
LEVELS = 32767.0
AHEAD = 2


def dft_block(m_column, row_shift, column_start, z, length, ra_per_device):
    rows = m_column.shape[0]
    column = lax.broadcasted_iota(jnp.int32, (rows, LANES), 1) + column_start
    part = column & 1
    per_source = 2 * ra_per_device
    source = column // per_source
    within = (column - source * per_source) >> 1
    t = source * (Z * ra_per_device) + z * ra_per_device + within
    quarter = length // 4
    phase = (m_column * t + (row_shift - part) * quarter) & (length - 1)
    wrapped = ((phase + length // 2) & (length - 1)) - length // 2
    u = quarter - jnp.abs(wrapped)
    x = u.astype(jnp.float32) * (2.0 * math.pi / length)
    x2 = x * x
    poly = jnp.float32(-1.0 / math.factorial(11))
    for order in (9, 7, 5, 3, 1):
        sign = 1.0 if order % 4 == 1 else -1.0
        poly = poly * x2 + jnp.float32(sign / math.factorial(order))
    return (x * poly * (1.0 / math.sqrt(length))).astype(jnp.bfloat16)


def kernel(
    length,
    vis,
    basis,
    eigen,
    kept,
    assigned,
    coeff_out,
    clean_out,
    recv,
    tail,
    table,
    part,
    zq,
    zs,
    zqr,
    zsr,
    fsend,
    spec,
    basis_v,
    basis_t,
    proj,
    eigen_v,
    assigned_v,
    basis_sem,
    small_sem,
    p1_send,
    p1_recv,
    zq_send,
    zq_recv,
    zs_send,
    zs_recv,
    f_send,
    f_recv,
    a_send,
    a_recv,
    answer,
):
    chunks, _, ra, _, _ = recv.shape
    nf, _, width = vis.shape[1:]
    quarter_width = chunks * WIDTH
    tail_width = tail.shape[-1]
    per_f = YX // nf
    ma = lax.axis_index("ma")
    af = lax.axis_index("af")
    yx = ma // Z
    z = ma % Z
    y, x = yx // SIDE, yx % SIDE

    def at_yx(other):
        return (other * Z + z, af)

    def at_z(other):
        return (yx * Z + other, af)

    def peer(step):
        dy, dx = step // SIDE, step % SIDE
        return ((y + dy) % SIDE) * SIDE + (x + dx) % SIDE

    def source(step):
        dy, dx = step // SIDE, step % SIDE
        return ((y + SIDE - dy) % SIDE) * SIDE + (x + SIDE - dx) % SIDE

    basis_copy = pltpu.make_async_copy(basis, basis_v, basis_sem)
    small_copies = [
        pltpu.make_async_copy(assigned, assigned_v, small_sem.at[0]),
        pltpu.make_async_copy(eigen, eigen_v, small_sem.at[1]),
    ]
    for copy in small_copies:
        copy.start()

    barrier = pltpu.get_barrier_semaphore()
    half, core = af // 2, af % 2
    role = half
    far = [(ma, (1 - half) * 2 + d) for d in (0, 1)]
    partners = [(ma, half * 2 + 1 - core)]
    partners += [at_z((z + d) % Z) for d in range(1, Z)]
    partners += [at_yx(peer(s)) for s in range(1, YX)]
    @pl.when(role == 1)
    def _():
        for partner in far:
            pl.semaphore_signal(barrier, inc=1, device_id=partner, device_id_type=MESH)

    for partner in partners:
        pl.semaphore_signal(barrier, inc=1, device_id=partner, device_id_type=MESH)

    def window(dest, k, wide):
        f, piece = dest // per_f, dest % per_f
        start = pl.multiple_of(piece * quarter_width + k * WIDTH, LANES)
        return vis.at[:, f, :, pl.ds(start, wide)]

    tail_start = (per_f - 1) * quarter_width + (chunks - 1) * WIDTH

    def tail_window(dest):
        return vis.at[:, dest // per_f, :, pl.ds(tail_start, tail_width)]

    is_tail = yx % per_f == per_f - 1
    for k in range(chunks):
        if k < chunks - 1:
            pltpu.make_async_copy(window(yx, k, WIDTH), recv.at[k, yx], p1_recv.at[k]).start()
        else:

            @pl.when(is_tail)
            def _():
                pltpu.make_async_copy(tail_window(yx), tail.at[yx], p1_recv.at[k]).start()

            @pl.when(jnp.logical_not(is_tail))
            def _():
                pltpu.make_async_copy(
                    window(yx, k, WIDTH), recv.at[k, yx], p1_recv.at[k]
                ).start()

    def each_piece(k, act, steps=tuple(range(1, YX))):
        for step in steps:
            if k < chunks - 1:
                act(step, k, False)
            else:
                to_tail = peer(step) % per_f == per_f - 1

                @pl.when(to_tail)
                def _():
                    act(step, k, True)

                @pl.when(jnp.logical_not(to_tail))
                def _():
                    act(step, k, False)

    @pl.when(role == 1)
    def _():
        pl.semaphore_wait(barrier, len(partners))

    @pl.when(role == 0)
    def _():
        pl.semaphore_wait(barrier, len(partners) + len(far))
        for partner in far:
            pl.semaphore_signal(answer, inc=1, device_id=partner, device_id_type=MESH)

    def p1(step, k, tailed):
        dest = peer(step)
        if tailed:
            src, dst = tail_window(dest), tail.at[yx]
        else:
            src, dst = window(dest, k, WIDTH), recv.at[k, yx]
        return pltpu.make_async_remote_copy(
            src_ref=src,
            dst_ref=dst,
            send_sem=p1_send.at[k, int(tailed)],
            recv_sem=p1_recv.at[k],
            device_id=at_yx(dest),
            device_id_type=MESH,
        )

    for k in range(min(AHEAD, chunks)):
        each_piece(k, lambda step, k, tailed: p1(step, k, tailed).start())

    basis_copy.start()

    rows = table.shape[0]
    row = lax.broadcasted_iota(jnp.int32, (rows, LANES), 0)
    lane = lax.broadcasted_iota(jnp.int32, (rows, LANES), 1)
    block = 2 * YX
    index = ((row % block) // 2) * Z + row // block
    small_copies[0].wait()
    chosen = jnp.where(lane == index, assigned_v[...].astype(jnp.float32), 0.0)
    m_column = jnp.sum(chosen, axis=1, keepdims=True).astype(jnp.int32)
    row_shift = row[:, :1] & 1
    for j in range(table.shape[1] // LANES):
        table[:, j * LANES : (j + 1) * LANES] = dft_block(
            m_column, row_shift, j * LANES, z, length, ra
        )

    basis_copy.wait()
    for f in range(nf):
        for c in range(2):
            basis_t[f, c] = basis_v[f, c].T

    def z_copies(d, k):
        target = dict(device_id=at_z((z + d) % Z), device_id_type=MESH)
        return [
            pltpu.make_async_remote_copy(
                src_ref=src.at[k, (z + d) % Z],
                dst_ref=dst.at[k, d - 1],
                send_sem=send.at[k],
                recv_sem=recv.at[k],
                **target,
            )
            for src, dst, send, recv in (
                (zs, zsr, zs_send, zs_recv),
                (zq, zqr, zq_send, zq_recv),
            )
        ]

    def rows_of(other):
        return pl.ds(pl.multiple_of(other * block, block), block)

    def arrived(ref, sem):
        pltpu.make_async_copy(ref, ref, sem).wait()

    def transform(k):
        def whole():
            arrived(recv.at[k], p1_recv.at[k])
            columns = recv[k].reshape(YX * 2 * ra, WIDTH)
            part[k] = jnp.dot(table[...], columns, preferred_element_type=jnp.float32)

        if k < chunks - 1:
            whole()
        else:

            @pl.when(is_tail)
            def _():
                arrived(tail, p1_recv.at[k])
                columns = tail[...].reshape(YX * 2 * ra, tail_width)
                part[k] = jnp.zeros_like(part[k])
                part[k, :, 0:tail_width] = jnp.dot(
                    table[...], columns, preferred_element_type=jnp.float32
                )

            @pl.when(jnp.logical_not(is_tail))
            def _():
                whole()

        pieces = part[k].reshape(Z, block, WIDTH)
        largest = jnp.maximum(jnp.max(jnp.abs(pieces), axis=1, keepdims=True), 1e-30)
        zs[k] = largest * (1.0 / LEVELS)
        zq[k] = jnp.round(pieces * (LEVELS / largest)).astype(jnp.int32).astype(jnp.int16)
        per_message = -(-(YX - 1) // (Z - 1))
        for i, d in enumerate(Z_STEPS):
            for copy in z_copies(d, k):
                copy.start()
            if k + AHEAD < chunks:
                each_piece(
                    k + AHEAD,
                    lambda step, k, tailed: p1(step, k, tailed).start(),
                    range(1, YX)[i * per_message : (i + 1) * per_message],
                )

    def place(src, k):
        start = pl.multiple_of((src % per_f) * quarter_width + k * WIDTH, LANES)
        return spec.at[src // per_f, :, pl.ds(start, WIDTH)]

    def f_local(k):
        return pltpu.make_async_copy(fsend.at[k, yx], place(yx, k), f_recv.at[k])

    def f_copy(step, k):
        dest = peer(step)
        return pltpu.make_async_remote_copy(
            src_ref=fsend.at[k, dest],
            dst_ref=place(yx, k),
            send_sem=f_send.at[k],
            recv_sem=f_recv.at[k],
            device_id=at_yx(dest),
            device_id_type=MESH,
        )

    def reduce(k):
        total = part[k, rows_of(z)]
        arrived(zsr.at[k], zs_recv.at[k])
        arrived(zqr.at[k], zq_recv.at[k])
        for d in Z_STEPS:
            total += zqr[k, d - 1].astype(jnp.float32) * zsr[k, d - 1]
        fsend[k] = total.reshape(YX, 2, WIDTH)
        f_local(k).start()
        for step in range(1, YX):
            f_copy(step, k).start()

    for k in range(chunks + 1):
        if k < chunks:
            transform(k)
        if k >= 1:
            reduce(k - 1)

    total = jnp.zeros((1, LANES), jnp.float32)
    for k in range(chunks):
        arrived(fsend.at[k], f_recv.at[k])
        for piece in range(per_f):
            start = piece * quarter_width + k * WIDTH
            stop = min(start + WIDTH, width)
            for f in range(nf):
                for c in range(2):
                    rounded = spec[f, c : c + 1, start:stop].astype(jnp.bfloat16)
                    total += jnp.dot(
                        rounded, basis_v[f, c, start:stop], preferred_element_type=jnp.float32
                    )
    proj[af] = total

    def a_copy(d):
        return pltpu.make_async_remote_copy(
            src_ref=proj.at[af],
            dst_ref=proj.at[af],
            send_sem=a_send.at[d - 1],
            recv_sem=a_recv.at[d - 1],
            device_id=(ma, (af + d) % 4),
            device_id_type=MESH,
        )

    @pl.when(role == 1)
    def _():
        pl.semaphore_wait(answer, len(far))

    for d in (2, 3, 1):
        a_copy(d).start()
    for k in range(chunks):
        if k < chunks - 1:
            arrived(recv.at[k, pl.ds(0, YX - 1)], p1_send.at[k, 0])
        else:

            @pl.when(is_tail)
            def _():
                arrived(recv.at[k, pl.ds(0, YX - nf)], p1_send.at[k, 0])
                arrived(tail.at[pl.ds(0, nf - 1)], p1_send.at[k, 1])

            @pl.when(jnp.logical_not(is_tail))
            def _():
                arrived(recv.at[k, pl.ds(0, YX - nf - 1)], p1_send.at[k, 0])
                arrived(tail.at[pl.ds(0, nf)], p1_send.at[k, 1])

        arrived(zsr.at[k], zs_send.at[k])
        arrived(zqr.at[k], zq_send.at[k])
        arrived(fsend.at[k, pl.ds(0, YX - 1)], f_send.at[k])
    for d in (1, 2, 3):
        a_copy(d).wait_recv()
    summed = proj[0] + proj[1] + proj[2] + proj[3]
    lanes = lax.broadcasted_iota(jnp.int32, (1, LANES), 1)
    small_copies[1].wait()
    keep = jnp.where(lanes < kept[0], 1.0, 0.0)
    gains = eigen_v[...] / (1.0 + eigen_v[...]) * keep
    coeffs = summed * gains
    coeff_out[...] = coeffs
    half_coeffs = coeffs.astype(jnp.bfloat16)
    for f in range(nf):
        for c in range(2):
            restored = jnp.dot(
                half_coeffs, basis_t[f, c], preferred_element_type=jnp.float32
            )
            clean_out[f, c : c + 1, :] = spec[f, c : c + 1, 0:width] - restored

    for d in (1, 2, 3):
        a_copy(d).wait_send()


def local(visibilities, kl_basis, eigenvalues, kept_modes, assigned_m):
    ra, nf, _, width = visibilities.shape
    length = ra * YX * Z
    modes = kl_basis.shape[-1]
    per_f = YX // nf
    chunks = -(-width // (per_f * WIDTH))
    tail_width = width - (per_f * chunks - 1) * WIDTH
    rows = 2 * assigned_m.shape[0]
    block = 2 * YX
    f32 = jnp.float32
    dma = pltpu.SemaphoreType.DMA
    vmem, smem, hbm = pltpu.VMEM, pltpu.SMEM, pltpu.HBM
    in_hbm = functools.partial(pltpu.with_memory_space_constraint, memory_space=hbm)
    coeffs, cleaned = pl.pallas_call(
        functools.partial(kernel, length),
        out_shape=(
            vmem((1, modes), f32),
            vmem((nf, 2, width), f32),
        ),
        in_specs=[pl.BlockSpec(memory_space=s) for s in (hbm, hbm, hbm, smem, hbm)],
        out_specs=(pl.BlockSpec(memory_space=vmem), pl.BlockSpec(memory_space=vmem)),
        scratch_shapes=[
            vmem((chunks, YX, ra, 2, WIDTH), jnp.bfloat16),
            vmem((YX, ra, 2, tail_width), jnp.bfloat16),
            vmem((rows, YX * ra * 2), jnp.bfloat16),
            vmem((chunks, rows, WIDTH), f32),
            vmem((chunks, Z, block, WIDTH), jnp.int16),
            vmem((chunks, Z, 1, WIDTH), f32),
            vmem((chunks, Z - 1, block, WIDTH), jnp.int16),
            vmem((chunks, Z - 1, 1, WIDTH), f32),
            vmem((chunks, YX, 2, WIDTH), f32),
            vmem((nf, 2, per_f * chunks * WIDTH), f32),
            vmem((nf, 2, width, modes), jnp.bfloat16),
            vmem((nf, 2, modes, width), jnp.bfloat16),
            vmem((4, 1, modes), f32),
            vmem((1, modes), f32),
            vmem((1, rows // 2), jnp.int32),
            dma,
            dma((2,)),
            dma((chunks, 2)),
            dma((chunks,)),
            dma((chunks,)),
            dma((chunks,)),
            dma((chunks,)),
            dma((chunks,)),
            dma((chunks,)),
            dma((chunks,)),
            dma((3,)),
            dma((3,)),
            pltpu.SemaphoreType.REGULAR,
        ],
        compiler_params=pltpu.CompilerParams(
            collective_id=0, has_side_effects=True, vmem_limit_bytes=40 << 20
        ),
    )(
        in_hbm(visibilities),
        in_hbm(kl_basis.reshape(nf, 2, width, modes)),
        in_hbm(eigenvalues),
        kept_modes,
        in_hbm(assigned_m.reshape(1, -1)),
    )
    return coeffs, cleaned[None]


def solution(mesh):
    in_specs = (
        P("ma", "af", None, None),
        P("ma", "af", None, None, None),
        P("ma", None),
        P("ma"),
        P(),
    )
    out_specs = (P("ma", None), P("ma", "af", None, None))
    return jax.shard_map(local, mesh=mesh, in_specs=in_specs, out_specs=out_specs, check_vma=False)
```
